256 devices in a mesh: inline: 8 (over x, z_lo), xline: 32 (over y, z_hi, core).
Axes of the slice: x: 4, y: 4, z: 8 (z_hi: 4, z_lo: 2; z = z_hi * 2 + z_lo), core: 2. Of those that a mesh axis runs over, the one named last changes fastest.
Arguments:
- traces: float32 [64, 512, 1024], P('inline', 'xline'), may hold values from -6 to 6
- filters: float32 [2, 512, 81], replicated, may hold values from -0.6 to 0.6
Outputs:
- denoised: float32 [64, 512, 1024], P('inline', 'xline')
The draws below stay inside these ranges and needn't reach their ends.
All inputs are finite; a program needn't handle non-finite values.
Results may differ from the reference program's by a relative error of at most 0.00007.
Values sent between devices are 32-bit elements; how exact they have to be, the bound alone decides.
No kernel may reach another device: no remote copies, remote signals or barrier semaphores. Data moves between devices by JAX's collectives and lax.ppermute only.
A program may use at most 64 MiB of HBM per device.

```python
import jax
import jax.numpy as jnp
from jax import lax

NT = 1024
NF = 512
NIL = 64
NXL = 512


def level_of(key, shape, split, smallest, largest):
    loudness, own = 1.0, jax.random.fold_in(key, 6)
    for position, shards_of in split:
        heights = jnp.exp(jax.random.uniform(jax.random.fold_in(own, position), (shards_of,), jnp.float32, smallest / len(split), largest / len(split)))
        loudness = loudness * jnp.repeat(heights, shape[position] // shards_of).reshape([-1 if axis == position else 1 for axis in range(len(shape))])
    return loudness


def gaussian(key, shape, spread, most, pieces=(), kind=jnp.bfloat16):
    gain = level_of(key, shape, pieces, -0.22, 0.18) if pieces else 1.0
    values = jax.random.normal(key, shape, jnp.float32) * spread * gain
    return jnp.minimum(jnp.maximum(values, -most), most).astype(kind)


def setup_inputs(seed: int = 0) -> dict:
    key_list = jax.random.split(jax.random.key(seed), 3)
    return {
        "traces": gaussian(key_list[0], (NIL, NXL, NT), 1.0, 6.0, ((0, 8), (1, 32)), jnp.float32),
        "filters": gaussian(key_list[1], (2, NF, 81), 0.1, 0.6, (), jnp.float32),
    }


def filter_bin(operands):
    plane_real, plane_imag, taps_real, taps_imag = operands
    rows_total = plane_real.shape[0]
    cols_total = plane_real.shape[1]
    padded_real = jnp.pad(plane_real, 4)
    padded_imag = jnp.pad(plane_imag, 4)
    total_real = jnp.zeros_like(plane_real)
    total_imag = jnp.zeros_like(plane_imag)
    for shift_row in range(9):
        for shift_col in range(9):
            index_tap = shift_row * 9 + shift_col
            piece_real = padded_real[shift_row:shift_row + rows_total, shift_col:shift_col + cols_total]
            piece_imag = padded_imag[shift_row:shift_row + rows_total, shift_col:shift_col + cols_total]
            total_real = total_real + taps_real[index_tap] * piece_real - taps_imag[index_tap] * piece_imag
            total_imag = total_imag + taps_real[index_tap] * piece_imag + taps_imag[index_tap] * piece_real
    return total_real, total_imag


def reference(traces, filters):
    spectrum = jnp.fft.rfft(traces, axis=-1)[:, :, :NF]
    spec_real = jnp.transpose(jnp.real(spectrum), (2, 0, 1))
    spec_imag = jnp.transpose(jnp.imag(spectrum), (2, 0, 1))
    out_real, out_imag = lax.map(filter_bin, (spec_real, spec_imag, filters[0], filters[1]))
    filtered = jnp.transpose(out_real, (1, 2, 0)) + 1j * jnp.transpose(out_imag, (1, 2, 0))
    full_bins = jnp.pad(filtered, ((0, 0), (0, 0), (0, NT // 2 + 1 - NF)))
    denoised = jnp.fft.irfft(full_bins, n=NT, axis=-1)
    return denoised.astype(jnp.float32)
```

```python
import math

import jax
import jax.numpy as jnp
import ml_dtypes
import numpy as np
from jax import lax
from jax.experimental import pallas as pl
from jax.experimental.pallas import tpu as pltpu
from jax.sharding import PartitionSpec as P

ROWS, COLS, NT = 8, 16, 1024
HALF = NT // 2
HALO = 4
TAPS = 9
OUTC = COLS + HALO
FRAME = 32
AXES = ("inline", "xline")


def split_bf16(table):
    high = table.astype(ml_dtypes.bfloat16)
    low = (table - high.astype(np.float64)).astype(ml_dtypes.bfloat16)
    return high, low


def tables():
    time_index = np.arange(HALF)[:, None]
    out = []
    for parity in (0, 1):
        bins = 2 * np.arange(HALF // 2)[None, :] + parity
        phase = (time_index * bins % NT) * (2.0 * math.pi / NT)
        table = np.concatenate([np.cos(phase), -np.sin(phase)], axis=1)
        out.extend(split_bf16(table))
    return np.stack(out)


SUBLANE = ((0, 1, 4, 5), (2, 3, 6, 7))


def high_low(x):
    high = x.astype(jnp.bfloat16)
    return high, (x - high.astype(jnp.float32)).astype(jnp.bfloat16)


def dot3(x, high, low, contract):
    dims = (((1,), (contract,)), ((), ()))
    xh, xl = high_low(x)
    dot = lambda a, b: lax.dot_general(a, b, dims, preferred_element_type=jnp.float32)
    return dot(xh, high) + (dot(xl, high) + dot(xh, low))


def forward(x, tab_ref):
    first, second = x[:, :HALF], x[:, HALF:]
    tiles = [None] * 8
    for parity, value in ((0, first + second), (1, first - second)):
        product = dot3(value, tab_ref[2 * parity], tab_ref[2 * parity + 1], 0)
        for c in range(4):
            tiles[SUBLANE[parity][c]] = product[:, c * 128 : (c + 1) * 128]
    return tiles


def place(tiles, start, count, ref, swapped_ref, base):
    for s in range(8):
        value = tiles[s][start : start + count]
        ref[pl.ds(base * 8 + s, count, stride=8), :] = value
        swapped_ref[pl.ds(base * 8 + (s ^ 4), count, stride=8), :] = value


def filter_row(tap_regs, in_base, out_base, count, ref, swapped_ref, acc_ref):
    acc = [acc_ref[pl.ds((out_base + t) * 8, 8), :] for t in range(count)]
    for e in range(count + TAPS - 1):
        offset = pl.ds((in_base + e) * 8, 8)
        x, xs = ref[offset, :], swapped_ref[offset, :]
        for b in range(TAPS):
            t = e - b
            if 0 <= t < count:
                acc[t] = acc[t] + (tap_regs[b] * x + tap_regs[TAPS + b] * xs)
    for t in range(count):
        acc_ref[pl.ds((out_base + t) * 8, 8), :] = acc[t]


def load_taps(h_ref, a):
    tap = lambda b, part: h_ref[pl.ds(((a * TAPS + b) * 2 + part) * 8, 8), :]
    return [tap(b, 0) for b in range(TAPS)] + [tap(b, 1) for b in range(TAPS)]


def parity_of(axis):
    return lax.rem(lax.axis_index(axis), 2)


def own_kernel(x_ref, side_ref, tab_ref, h_ref, acc_ref, fr, fs, tmp, tmps):
    odd = parity_of("xline")
    column = lax.axis_index("xline")
    is_edge = (column == 0) | (column == lax.axis_size("xline") - 1)
    keep = jnp.where(is_edge, 0.0, 1.0).astype(jnp.float32)
    zero = jnp.zeros((8 * 8, 128), jnp.float32)
    for i in range(ROWS):
        for base in (i * FRAME, i * FRAME + 24):
            fr[pl.ds(base * 8, 64), :] = zero
            fs[pl.ds(base * 8, 64), :] = zero
    tiles = forward(x_ref[...].reshape(ROWS * COLS, NT), tab_ref)
    for i in range(ROWS):
        place(tiles, i * COLS, COLS, fr, fs, i * FRAME + 8)
    side_tiles = forward(side_ref[...], tab_ref)
    place(side_tiles, 0, ROWS * HALO, tmp, tmps, 0)
    side_base = 4 + 20 * odd
    for i in range(ROWS):
        source = pl.ds(i * HALO * 8, HALO * 8)
        target = pl.ds(pl.multiple_of((i * FRAME + side_base) * 8, 8), HALO * 8)
        fr[target, :] = tmp[source, :] * keep
        fs[target, :] = tmps[source, :] * keep
    acc_ref[...] = jnp.zeros_like(acc_ref)
    in_col = HALO - HALO * odd

    def tap_row(a, carry):
        regs = load_taps(h_ref, a)

        def out_row(i, carry):
            for t0 in range(0, OUTC, 10):
                filter_row(regs, (i + a - HALO) * FRAME + in_col + t0, i * OUTC + t0, 10, fr, fs, acc_ref)
            return carry

        return lax.fori_loop(jnp.maximum(0, HALO - a), jnp.minimum(ROWS, ROWS + HALO - a), out_row, carry)

    lax.fori_loop(0, TAPS, tap_row, 0)


def rows_kernel(acc_in, near_ref, far_ref, tab_ref, h_ref, acc_ref, mate_ref, work, fr, fs):
    odd_row, odd = parity_of("inline"), parity_of("xline")
    row = lax.axis_index("inline")
    is_edge = (row == 0) | (row == lax.axis_size("inline") - 1)
    keep = jnp.where(is_edge, 0.0, 1.0).astype(jnp.float32)
    work[...] = acc_in[...]
    zero = jnp.zeros((8 * 8, 128), jnp.float32)
    for i in range(ROWS):
        for base in (i * FRAME, i * FRAME + 24):
            fr[pl.ds(base * 8, 64), :] = zero
            fs[pl.ds(base * 8, 64), :] = zero
    near_tiles = forward(near_ref[...].reshape(HALO * COLS, NT), tab_ref)
    far_tiles = [tile * keep for tile in forward(far_ref[...].reshape(HALO * COLS, NT), tab_ref)]
    is_odd = odd_row == 1
    above = [jnp.where(is_odd, n, f) for n, f in zip(near_tiles, far_tiles)]
    below = [jnp.where(is_odd, f, n) for n, f in zip(near_tiles, far_tiles)]
    for r in range(HALO):
        place(above, r * COLS, COLS, fr, fs, r * FRAME + 8)
        place(below, r * COLS, COLS, fr, fs, (HALO + r) * FRAME + 8)
    in_col = HALO - HALO * odd

    for a in (0, 1, 2, 3, 5, 6, 7, 8):
        regs = load_taps(h_ref, a)

        def out_row(i, carry):
            in_row = i + a if a < HALO else i + a - 2 * HALO
            for t0 in range(0, OUTC, 10):
                filter_row(regs, in_row * FRAME + in_col + t0, i * OUTC + t0, 10, fr, fs, work)
            return carry

        if a < HALO:
            lax.fori_loop(0, HALO - a, out_row, 0)
        else:
            lax.fori_loop(ROWS + HALO - a, ROWS, out_row, 0)
    for i in range(ROWS):
        own = pl.ds(pl.multiple_of((i * OUTC + HALO * odd) * 8, 8), COLS * 8)
        acc_ref[pl.ds(i * COLS * 8, COLS * 8), :] = work[own, :]
        mate = pl.ds(pl.multiple_of((i * OUTC + COLS - COLS * odd) * 8, 8), HALO * 8)
        mate_ref[pl.ds(i * HALO * 8, HALO * 8), :] = work[mate, :]


def last_kernel(acc_in, mate_ref, near_ref, far_ref, tab_ref, h_ref, out_ref, work, fr, fs, tmp, tmps):
    odd_row, odd = parity_of("inline"), parity_of("xline")
    row, column = lax.axis_index("inline"), lax.axis_index("xline")
    row_edge = (row == 0) | (row == lax.axis_size("inline") - 1)
    column_edge = (column == 0) | (column == lax.axis_size("xline") - 1)
    keep_near = jnp.where(column_edge, 0.0, 1.0).astype(jnp.float32)
    keep_far = jnp.where(row_edge, 0.0, keep_near)
    work[...] = acc_in[...]
    fr[...] = jnp.zeros_like(fr)
    fs[...] = jnp.zeros_like(fs)
    corner = jnp.concatenate([near_ref[...], far_ref[...]], axis=0)
    place(forward(corner, tab_ref), 0, 2 * HALO * HALO, tmp, tmps, 0)
    for half, keep in ((0, keep_near), (1, keep_far)):
        first = HALO * (1 - odd_row) if half == 0 else HALO * odd_row
        for r in range(HALO):
            source = pl.ds((half * HALO + r) * HALO * 8, HALO * 8)
            target = pl.ds(pl.multiple_of(((first + r) * 12 + 8 * odd) * 8, 8), HALO * 8)
            fr[target, :] = tmp[source, :] * keep
            fs[target, :] = tmps[source, :] * keep
    out_col = 12 * odd
    for a in (0, 1, 2, 3, 5, 6, 7, 8):
        regs = load_taps(h_ref, a)

        def out_row(i, carry):
            in_row = i + a if a < HALO else i + a - 2 * HALO
            filter_row(regs, in_row * 12, i * COLS + out_col, HALO, fr, fs, work)
            return carry

        if a < HALO:
            lax.fori_loop(0, HALO - a, out_row, 0)
        else:
            lax.fori_loop(ROWS + HALO - a, ROWS, out_row, 0)
    for i in range(ROWS):
        target = pl.ds(pl.multiple_of((i * COLS + 12 - 12 * odd) * 8, 8), HALO * 8)
        work[target, :] = work[target, :] + mate_ref[pl.ds(i * HALO * 8, HALO * 8), :]
    lane = lax.broadcasted_iota(jnp.int32, (ROWS * COLS, 128), 1)
    parts = []
    for parity in (0, 1):
        tiles = [work[pl.ds(s, ROWS * COLS, stride=8), :] for s in SUBLANE[parity]]
        if parity == 0:
            tiles[0] = jnp.where(lane == 0, 0.5 * tiles[0], tiles[0])
        spectrum = jnp.concatenate(tiles, axis=1)
        parts.append(dot3(spectrum, tab_ref[2 * parity], tab_ref[2 * parity + 1], 1) * (2.0 / NT))
    out_ref[:, :, :HALF] = (parts[0] + parts[1]).reshape(ROWS, COLS, HALF)
    out_ref[:, :, HALF:] = (parts[0] - parts[1]).reshape(ROWS, COLS, HALF)


def call(kernel, outs, scratch, args):
    return pl.pallas_call(
        kernel,
        out_shape=[jax.ShapeDtypeStruct(shape, jnp.float32) for shape in outs],
        scratch_shapes=[pltpu.VMEM(shape, jnp.float32) for shape in scratch],
        compiler_params=pltpu.CompilerParams(vmem_limit_bytes=40 * 2**20),
    )(*args)


def permutations(inline, xline):
    number = lambda i, j: i * xline + j
    side, far = [], []
    for i in range(inline):
        for j in range(xline):
            k = j - 1 if j % 2 == 0 else j + 1
            side.append((number(i, j), number(i, k) if 0 <= k < xline else number(i ^ 1, j)))
            k = i - 1 if i % 2 == 0 else i + 1
            far.append((number(i, j), number(k, j) if 0 <= k < inline else number(i, j ^ 1)))
    near = [(i, i ^ 1) for i in range(inline)]
    mate = [(j, j ^ 1) for j in range(xline)]
    return side, far, near, mate


def per_device(traces, filters):
    side, far, near, mate = permutations(lax.axis_size("inline"), lax.axis_size("xline"))
    odd_row, odd = parity_of("inline"), parity_of("xline")
    tab = jnp.asarray(tables())

    edge = lax.dynamic_slice_in_dim(traces, 12 * odd, HALO, 1).reshape(ROWS * HALO, NT)
    edge, traces = lax.optimization_barrier((edge, traces))
    from_side = lax.ppermute(edge, AXES, side)
    to_near = lax.dynamic_slice_in_dim(traces, HALO - HALO * odd_row, HALO, 0)
    to_far = lax.dynamic_slice_in_dim(traces, HALO * odd_row, HALO, 0)
    from_far = lax.ppermute(to_far, AXES, far)
    from_near = lax.ppermute(to_near, "inline", near)
    corner = HALO * HALO
    corner_far = lax.ppermute(lax.dynamic_slice_in_dim(from_side, corner * odd_row, corner, 0), AXES, far)
    corner_near = lax.ppermute(lax.dynamic_slice_in_dim(from_side, corner - corner * odd_row, corner, 0), "inline", near)

    h = jnp.transpose(filters.reshape(2, HALF // 2, 2, TAPS * TAPS), (0, 3, 2, 1)).reshape(2, TAPS * TAPS, 4, 128)
    h = jnp.stack([jnp.concatenate([h[0], h[0]], 1), jnp.concatenate([-h[1], h[1]], 1)], 1)
    h = h.reshape(TAPS * TAPS * 16, 128)

    frame = (ROWS * FRAME * 8, 128)
    spot = (ROWS * HALO * 8, 128)
    (acc,) = call(own_kernel, [(ROWS * OUTC * 8, 128)], [frame, frame, spot, spot], (traces, from_side, tab, h))
    acc, to_mate = call(
        rows_kernel,
        [(ROWS * COLS * 8, 128), spot],
        [(ROWS * OUTC * 8, 128), frame, frame],
        (acc, from_near, from_far, tab, h),
    )
    from_mate = lax.ppermute(to_mate, "xline", mate)
    corner_frame = (ROWS * 12 * 8, 128)
    (out,) = call(
        last_kernel,
        [(ROWS, COLS, NT)],
        [(ROWS * COLS * 8, 128), corner_frame, corner_frame, spot, spot],
        (acc, from_mate, corner_near, corner_far, tab, h),
    )
    return out


def solution(mesh):
    return jax.shard_map(
        per_device,
        mesh=mesh,
        in_specs=(P("inline", "xline", None), P()),
        out_specs=P("inline", "xline", None),
        check_vma=False,
    )
```

```python
import math

import jax
import jax.numpy as jnp
import ml_dtypes
import numpy as np
from jax import lax
from jax.experimental import pallas as pl
from jax.experimental.pallas import tpu as pltpu
from jax.sharding import PartitionSpec as P

ROWS, COLS, NT = 8, 16, 1024
HALF = NT // 2
HALO = 4
TAPS = 9
WIDE = COLS + HALO
AXES = ("inline", "xline")
OUTER_ROWS = (0, 1, 2, 3, 5, 6, 7, 8)


def split_bf16(table):
    high = table.astype(ml_dtypes.bfloat16)
    low = (table - high.astype(np.float64)).astype(ml_dtypes.bfloat16)
    return high, low


def tables():
    time_index = np.arange(HALF)[:, None]
    out = []
    for parity in (0, 1):
        bins = 2 * np.arange(HALF // 2)[None, :] + parity
        phase = (time_index * bins % NT) * (2.0 * math.pi / NT)
        table = np.concatenate([np.cos(phase), -np.sin(phase)], axis=1)
        out.extend(split_bf16(table))
    return np.stack(out)


def bin_order():
    order = np.concatenate([np.arange(0, HALF, 2), np.arange(1, HALF, 2)])
    return (np.arange(HALF)[:, None] == order[None, :]).astype(ml_dtypes.bfloat16)


SUBLANE = ((0, 1, 4, 5), (2, 3, 6, 7))


def dot(a, b, contract=0):
    return lax.dot_general(a, b, (((1,), (contract,)), ((), ())), preferred_element_type=jnp.float32)


def high_low(x):
    high = x.astype(jnp.bfloat16)
    return high, (x - high.astype(jnp.float32)).astype(jnp.bfloat16)


def dot3(x, high, low, contract):
    xh, xl = high_low(x)
    return dot(xh, high, contract) + (dot(xl, high, contract) + dot(xh, low, contract))


def forward(x, tab_ref):
    first, second = x[:, :HALF], x[:, HALF:]
    tiles = [None] * 8
    for parity, value in ((0, first + second), (1, first - second)):
        product = dot3(value, tab_ref[2 * parity], tab_ref[2 * parity + 1], 0)
        for c in range(4):
            tiles[SUBLANE[parity][c]] = product[:, c * 128 : (c + 1) * 128]
    return tiles


def place(tiles, start, count, ref, swapped_ref, base):
    for s in range(8):
        value = tiles[s][start : start + count]
        ref[pl.ds(base * 8 + s, count, stride=8), :] = value
        swapped_ref[pl.ds(base * 8 + (s ^ 4), count, stride=8), :] = value


def filter_row(regs, ref, swapped_ref, in_base, inputs, acc_ref, out_base, outputs, shift):
    spot = lambda base, n: pl.ds((base + n) * 8, 8)
    acc = {t: acc_ref[spot(out_base, t), :] for t in outputs}
    for n in inputs:
        pairs = [(n - b + shift, b) for b in range(TAPS) if n - b + shift in acc]
        if pairs:
            x, xs = ref[spot(in_base, n - inputs[0]), :], swapped_ref[spot(in_base, n - inputs[0]), :]
            for t, b in pairs:
                acc[t] = acc[t] + (regs[b] * x + regs[TAPS + b] * xs)
    for t in outputs:
        acc_ref[spot(out_base, t), :] = acc[t]


def load_taps(h_ref, a):
    tap = lambda b, part: h_ref[pl.ds(((a * TAPS + b) * 2 + part) * 8, 8), :]
    return [tap(b, 0) for b in range(TAPS)] + [tap(b, 1) for b in range(TAPS)]


def parity_of(axis):
    return lax.rem(lax.axis_index(axis), 2)


def keep_of(axis):
    index = lax.axis_index(axis)
    is_end = (index == 0) | (index == lax.axis_size(axis) - 1)
    return jnp.where(is_end, 0.0, 1.0).astype(jnp.float32)


def each_parity(body):
    odd = parity_of("xline")
    for parity in (0, 1):
        pl.when(odd == parity)(lambda: body(parity))


def edges_kernel(x_ref, edge_ref, far_ref, near_ref):
    odd_row = parity_of("inline")

    def body(parity):
        first = 12 * parity
        for i in range(ROWS):
            row = lax.rem(i + HALO * odd_row, ROWS)
            edge_ref[i * HALO : (i + 1) * HALO, :] = x_ref[row, first : first + HALO, :]

    each_parity(body)
    for r in range(HALO):
        far_ref[r * COLS : (r + 1) * COLS, :] = x_ref[HALO * odd_row + r]
        near_ref[r * COLS : (r + 1) * COLS, :] = x_ref[HALO - HALO * odd_row + r]


def taps_kernel(f_ref, order_ref, x_ref, tab_ref, h_ref):
    rest, taps = f_ref[...], 0.0
    for _ in range(3):
        part = rest.astype(jnp.bfloat16)
        rest = rest - part.astype(jnp.float32)
        taps = taps + dot(part, order_ref[...])
    count = 2 * TAPS * TAPS
    is_imag = lax.rem(lax.broadcasted_iota(jnp.int32, (count, 128), 0), 2) == 1
    for s in range(4):
        value = taps[:, s * 128 : (s + 1) * 128]
        h_ref[pl.ds(s, count, stride=8), :] = jnp.where(is_imag, -value, value)
        h_ref[pl.ds(s + 4, count, stride=8), :] = value


def corners_kernel(side_ref, h_ref, far_ref, near_ref):
    far_ref[...] = side_ref[: HALO * HALO, :]
    near_ref[...] = side_ref[HALO * HALO :, :]


def own_kernel(x_ref, side_ref, tab_ref, h_ref, acc_ref, fr, fs, tmp, tmps):
    odd_row = parity_of("inline")
    keep = keep_of("xline")
    tiles = forward(x_ref[...].reshape(ROWS * COLS, NT), tab_ref)
    place(forward(side_ref[...], tab_ref), 0, ROWS * HALO, tmp, tmps, 0)
    acc_ref[...] = jnp.zeros_like(acc_ref)

    def body(parity):
        side_first = COLS * parity
        for i in range(ROWS):
            place(tiles, i * COLS, COLS, fr, fs, i * WIDE + HALO - HALO * parity)
            row = lax.rem(i + HALO * odd_row, ROWS)
            source = pl.ds(i * HALO * 8, HALO * 8)
            target = pl.ds(pl.multiple_of((row * WIDE + side_first) * 8, 8), HALO * 8)
            fr[target, :] = tmp[source, :] * keep
            fs[target, :] = tmps[source, :] * keep

        def tap_row(a, carry):
            regs = load_taps(h_ref, a)

            def out_row(i, carry):
                for t0 in (0, WIDE // 2):
                    outputs = range(t0, t0 + WIDE // 2)
                    filter_row(
                        regs, fr, fs, (i + a - HALO) * WIDE, range(WIDE), acc_ref, i * WIDE, outputs, 8 * parity
                    )
                return carry

            return lax.fori_loop(jnp.maximum(0, HALO - a), jnp.minimum(ROWS, ROWS + HALO - a), out_row, carry)

        lax.fori_loop(0, TAPS, tap_row, 0)

    each_parity(body)


def outer_rows(h_ref, body):
    for a in OUTER_ROWS:
        regs = load_taps(h_ref, a)
        above = a < HALO

        def out_row(i, carry):
            body(regs, i + a if above else i + a - 2 * HALO, i)
            return carry

        lax.fori_loop(0 if above else ROWS + HALO - a, HALO - a if above else ROWS, out_row, 0)


def rows_kernel(acc_ref, near_ref, far_ref, tab_ref, h_ref, mate_ref, fr, fs):
    odd_row = parity_of("inline")
    keep = keep_of("inline")
    near_tiles = forward(near_ref[...], tab_ref)
    far_tiles = [tile * keep for tile in forward(far_ref[...], tab_ref)]
    is_odd = odd_row == 1
    above = [jnp.where(is_odd, n, f) for n, f in zip(near_tiles, far_tiles)]
    below = [jnp.where(is_odd, f, n) for n, f in zip(near_tiles, far_tiles)]
    place(above, 0, HALO * COLS, fr, fs, 0)
    place(below, 0, HALO * COLS, fr, fs, HALO * COLS)

    def body(parity):
        first = COLS - COLS * parity
        for i in range(ROWS):
            mate_ref[pl.ds(i * HALO * 8, HALO * 8), :] = acc_ref[pl.ds((i * WIDE + first) * 8, HALO * 8), :]
        inputs = range(COLS, WIDE) if parity == 0 else range(0, HALO)
        skip = COLS - HALO if parity == 0 else 0
        shift = 8 * parity - first

        def filter_out(regs, frame_row, i):
            filter_row(
                regs, fr, fs, frame_row * COLS + skip, inputs, mate_ref, i * HALO, range(HALO), shift
            )

        outer_rows(h_ref, filter_out)

    each_parity(body)


def inner_kernel(acc_ref, fr, fs, near_ref, far_ref, tab_ref, h_ref, out_ref, cr, cs, tmp, tmps):
    odd_row = parity_of("inline")
    keep_near = keep_of("xline")
    keep_far = keep_near * keep_of("inline")
    corner = jnp.concatenate([near_ref[...], far_ref[...]], axis=0)
    place(forward(corner, tab_ref), 0, 2 * HALO * HALO, tmp, tmps, 0)
    size = HALO * HALO * 8
    for half, keep in ((0, keep_near), (1, keep_far)):
        first = 1 - odd_row if half == 0 else odd_row
        source, target = pl.ds(half * size, size), pl.ds(pl.multiple_of(first * size, 8), size)
        cr[target, :] = tmp[source, :] * keep
        cs[target, :] = tmps[source, :] * keep

    def body(parity):
        own = HALO * parity
        for i in range(ROWS):
            out_ref[pl.ds(i * COLS * 8, COLS * 8), :] = acc_ref[pl.ds((i * WIDE + own) * 8, COLS * 8), :]
        inputs = range(HALO - own, WIDE - own)
        side = range(0, HALO) if parity == 0 else range(COLS, WIDE)
        near_side = range(0, HALO) if parity == 0 else range(COLS - HALO, COLS)
        shift = 8 * parity - own

        def filter_out(regs, frame_row, i):
            for t0 in (0, COLS // 2):
                filter_row(
                    regs, fr, fs, frame_row * COLS, inputs, out_ref, i * COLS, range(t0, t0 + COLS // 2), shift
                )
            filter_row(regs, cr, cs, frame_row * HALO, side, out_ref, i * COLS, near_side, shift)

        outer_rows(h_ref, filter_out)

    each_parity(body)


def inverse_kernel(acc_ref, mate_ref, tab_ref, out_ref, work):
    odd = parity_of("xline")
    work[...] = acc_ref[...]
    for i in range(ROWS):
        target = pl.ds(pl.multiple_of((i * COLS + 12 - 12 * odd) * 8, 8), HALO * 8)
        work[target, :] = work[target, :] + mate_ref[pl.ds(i * HALO * 8, HALO * 8), :]
    lane = lax.broadcasted_iota(jnp.int32, (ROWS * COLS, 128), 1)
    parts = []
    for parity in (0, 1):
        tiles = [work[pl.ds(s, ROWS * COLS, stride=8), :] for s in SUBLANE[parity]]
        if parity == 0:
            tiles[0] = jnp.where(lane == 0, 0.5 * tiles[0], tiles[0])
        spectrum = jnp.concatenate(tiles, axis=1)
        parts.append(dot3(spectrum, tab_ref[2 * parity], tab_ref[2 * parity + 1], 1) * (2.0 / NT))
    out_ref[:, :, :HALF] = (parts[0] + parts[1]).reshape(ROWS, COLS, HALF)
    out_ref[:, :, HALF:] = (parts[0] - parts[1]).reshape(ROWS, COLS, HALF)


def call(kernel, outs, scratch, args, specs=None, weight=0):
    return pl.pallas_call(
        kernel,
        out_shape=[jax.ShapeDtypeStruct(shape, jnp.float32) for shape in outs],
        in_specs=specs or [pl.BlockSpec()] * len(args),
        scratch_shapes=[pltpu.VMEM(shape, jnp.float32) for shape in scratch],
        compiler_params=pltpu.CompilerParams(vmem_limit_bytes=40 * 2**20),
        cost_estimate=pl.CostEstimate(flops=weight * 10**9, bytes_accessed=0, transcendentals=0) if weight else None,
    )(*args)


def permutations(inline, xline):
    number = lambda i, j: i * xline + j
    side, far = [], []
    for i in range(inline):
        for j in range(xline):
            k = j - 1 if j % 2 == 0 else j + 1
            side.append((number(i, j), number(i, k) if 0 <= k < xline else number(i ^ 1, j)))
            k = i - 1 if i % 2 == 0 else i + 1
            far.append((number(i, j), number(k, j) if 0 <= k < inline else number(i, j ^ 1)))
    near = [(i, i ^ 1) for i in range(inline)]
    mate = [(j, j ^ 1) for j in range(xline)]
    return side, far, near, mate


def per_device(traces, filters):
    side, far, near, mate = permutations(lax.axis_size("inline"), lax.axis_size("xline"))
    tab = jnp.asarray(tables())
    taps = jnp.transpose(filters, (2, 0, 1)).reshape(2 * TAPS * TAPS, HALF)

    rows = (HALO * COLS, NT)
    corner = HALO * HALO
    edge, to_far, to_near = call(edges_kernel, [(ROWS * HALO, NT), rows, rows], [], (traces,))
    from_side = lax.ppermute(edge, AXES, side)
    from_far = lax.ppermute(to_far, AXES, far)
    from_near = lax.ppermute(to_near, "inline", near)
    vmem, anywhere = pl.BlockSpec(memory_space=pltpu.VMEM), pl.BlockSpec(memory_space=pl.ANY)
    (h,) = call(
        taps_kernel, [(2 * TAPS * TAPS * 8, 128)], [], (taps, jnp.asarray(bin_order()), traces, tab), weight=1
    )
    for_far, for_near = call(corners_kernel, [(corner, NT)] * 2, [], (from_side, h), [vmem, anywhere])
    corner_far = lax.ppermute(for_far, AXES, far)
    corner_near = lax.ppermute(for_near, "inline", near)

    wide = (ROWS * WIDE * 8, 128)
    frame = (ROWS * COLS * 8, 128)
    spot = (ROWS * HALO * 8, 128)
    (acc,) = call(own_kernel, [wide], [wide, wide, spot, spot], (traces, from_side, tab, h), weight=10)
    to_mate, fr, fs = call(rows_kernel, [spot, frame, frame], [], (acc, from_near, from_far, tab, h))
    from_mate = lax.ppermute(to_mate, "xline", mate)
    (acc,) = call(inner_kernel, [frame], [spot] * 4, (acc, fr, fs, corner_near, corner_far, tab, h), weight=10)
    (out,) = call(inverse_kernel, [(ROWS, COLS, NT)], [frame], (acc, from_mate, tab))
    return out


def solution(mesh):
    return jax.shard_map(
        per_device,
        mesh=mesh,
        in_specs=(P("inline", "xline", None), P()),
        out_specs=P("inline", "xline", None),
        check_vma=False,
    )
```

```python
import math

import jax
import jax.numpy as jnp
import ml_dtypes
import numpy as np
from jax import lax
from jax.experimental import pallas as pl
from jax.experimental.pallas import tpu as pltpu
from jax.sharding import PartitionSpec as P

ROWS, COLS, NT = 8, 16, 1024
HALF = NT // 2
HALO = 4
TAPS = 9
WIDE = COLS + 2 * HALO
CHUNK = 12
AXES = ("inline", "xline")


def split_bf16(table):
    high = table.astype(ml_dtypes.bfloat16)
    low = (table - high.astype(np.float64)).astype(ml_dtypes.bfloat16)
    return high, low


def tables():
    time_index = np.arange(HALF)[:, None]
    out, transposed = [], []
    for parity in (0, 1):
        bins = 2 * np.arange(HALF // 2)[None, :] + parity
        phase = (time_index * bins % NT) * (2.0 * math.pi / NT)
        table = np.concatenate([np.cos(phase), -np.sin(phase)], axis=1)
        out.extend(split_bf16(table))
        transposed.extend(split_bf16(table.T))
    return np.stack(out), np.stack(transposed)


SUBLANE = ((0, 1, 4, 5), (2, 3, 6, 7))


def dot(a, b):
    return lax.dot_general(a, b, (((1,), (0,)), ((), ())), preferred_element_type=jnp.float32)


def high_low(x):
    high = x.astype(jnp.bfloat16)
    return high, (x - high.astype(jnp.float32)).astype(jnp.bfloat16)


def dot3(x, high, low):
    xh, xl = high_low(x)
    return dot(xh, high) + (dot(xl, high) + dot(xh, low))


def forward(x, tab_ref):
    first, second = x[:, :HALF], x[:, HALF:]
    tiles = [None] * 8
    for parity, value in ((0, first + second), (1, first - second)):
        product = dot3(value, tab_ref[2 * parity], tab_ref[2 * parity + 1])
        for c in range(4):
            tiles[SUBLANE[parity][c]] = product[:, c * 128 : (c + 1) * 128]
    return tiles


def place(tiles, start, count, ref, swapped_ref, base):
    for s in range(8):
        value = tiles[s][start : start + count]
        ref[pl.ds(base * 8 + s, count, stride=8), :] = value
        swapped_ref[pl.ds(base * 8 + (s ^ 4), count, stride=8), :] = value


def filter_row(regs, ref, swapped_ref, in_base, inputs, acc_ref, out_base, outputs):
    spot = lambda base, n: pl.ds((base + n) * 8, 8)
    acc = {t: acc_ref[spot(out_base, t), :] for t in outputs}
    for n in inputs:
        pairs = [(n - b + 2 * HALO, b) for b in range(TAPS) if n - b + 2 * HALO in acc]
        if pairs:
            x, xs = ref[spot(in_base, n), :], swapped_ref[spot(in_base, n), :]
            for t, b in pairs:
                acc[t] = acc[t] + (regs[b] * x + regs[TAPS + b] * xs)
    for t in outputs:
        acc_ref[spot(out_base, t), :] = acc[t]


def load_taps(h_ref, a):
    tap = lambda b, part: h_ref[pl.ds(((a * TAPS + b) * 2 + part) * 8, 8), :]
    return [tap(b, 0) for b in range(TAPS)] + [tap(b, 1) for b in range(TAPS)]


def parity_of(axis):
    return lax.rem(lax.axis_index(axis), 2)


def keep_of(axis):
    index = lax.axis_index(axis)
    is_end = (index == 0) | (index == lax.axis_size(axis) - 1)
    return jnp.where(is_end, 0.0, 1.0).astype(jnp.float32)


def edges_kernel(x_ref, far_ref, near_ref):
    odd_row = parity_of("inline")
    for r in range(HALO):
        far_ref[r * COLS : (r + 1) * COLS, :] = x_ref[HALO * odd_row + r]
        near_ref[r * COLS : (r + 1) * COLS, :] = x_ref[HALO - HALO * odd_row + r]


def taps_kernel(f_ref, h_ref):
    source = lax.broadcasted_iota(jnp.int32, (HALF, HALF), 0)
    target = lax.broadcasted_iota(jnp.int32, (HALF, HALF), 1)
    wanted = jnp.where(target < HALF // 2, 2 * target, 2 * target - (HALF - 1))
    order = jnp.where(source == wanted, 1.0, 0.0).astype(jnp.bfloat16)
    count = TAPS * TAPS
    for part in (0, 1):
        rest = jnp.concatenate([f_ref[pl.ds(2 * tile + part, count, stride=8), :] for tile in range(4)], axis=1)
        taps = 0.0
        for _ in range(3):
            piece = rest.astype(jnp.bfloat16)
            rest = rest - piece.astype(jnp.float32)
            taps = taps + dot(piece, order)
        for s in range(4):
            value = taps[:, s * 128 : (s + 1) * 128]
            h_ref[pl.ds(part * 8 + s, count, stride=16), :] = -value if part else value
            h_ref[pl.ds(part * 8 + s + 4, count, stride=16), :] = value


def filter_columns(regs, fr, fs, row, acc_ref, i):
    for t0 in range(0, WIDE, CHUNK):
        filter_row(regs, fr, fs, row * COLS, range(COLS), acc_ref, i * WIDE, range(t0, t0 + CHUNK))


def own_kernel(x_ref, tab_ref, h_ref, acc_ref, fr, fs):
    place(forward(x_ref[...].reshape(ROWS * COLS, NT), tab_ref), 0, ROWS * COLS, fr, fs, 0)
    acc_ref[...] = jnp.zeros_like(acc_ref)

    def tap_row(a, carry):
        regs = load_taps(h_ref, a)

        def out_row(i, carry):
            filter_columns(regs, fr, fs, i + a - HALO, acc_ref, i)
            return carry

        return lax.fori_loop(jnp.maximum(0, HALO - a), jnp.minimum(ROWS, ROWS + HALO - a), out_row, carry)

    lax.fori_loop(0, TAPS, tap_row, 0)


def neighbour_rows(h_ref, below, body):
    for step in range(HALO):
        regs = load_taps(h_ref, step + (HALO + 1) * below)

        def out_row(i, carry):
            body(regs, i + step - 7 * below, i)
            return carry

        first = (ROWS - 1 - step) * below
        lax.fori_loop(first, HALO - step + (HALO + step) * below, out_row, 0)


def near_kernel(acc_in, near_ref, tab_ref, h_ref, acc_ref, fr, fs):
    acc_ref[...] = acc_in[...]
    place(forward(near_ref[...], tab_ref), 0, HALO * COLS, fr, fs, 0)
    neighbour_rows(
        h_ref, 1 - parity_of("inline"), lambda regs, row, i: filter_columns(regs, fr, fs, row, acc_ref, i)
    )


def ends_kernel(acc_ref, far_ref, tab_ref, h_ref, side_ref, mate_ref, fr, fs):
    keep = keep_of("inline")
    tiles = [tile * keep for tile in forward(far_ref[...], tab_ref)]
    place(tiles, 0, HALO * COLS, fr, fs, 0)

    def body(parity):
        left_ref, right_ref = (side_ref, mate_ref) if parity == 0 else (mate_ref, side_ref)
        right = WIDE - HALO
        for i in range(ROWS):
            target = pl.ds(i * HALO * 8, HALO * 8)
            left_ref[target, :] = acc_ref[pl.ds(i * WIDE * 8, HALO * 8), :]
            right_ref[target, :] = acc_ref[pl.ds((i * WIDE + right) * 8, HALO * 8), :]

        def far_out(regs, row, i):
            base = row * COLS
            filter_row(regs, fr, fs, base, range(HALO), left_ref, i * HALO, range(HALO))
            filter_row(
                regs, fr, fs, base, range(COLS - HALO, COLS), right_ref, i * HALO - right, range(right, WIDE)
            )

        neighbour_rows(h_ref, parity_of("inline"), far_out)

    odd = parity_of("xline")
    for parity in (0, 1):
        pl.when(odd == parity)(lambda: body(parity))


def inner_kernel(acc_ref, fr, fs, h_ref, out_ref):
    for i in range(ROWS):
        out_ref[pl.ds(i * COLS * 8, COLS * 8), :] = acc_ref[pl.ds((i * WIDE + HALO) * 8, COLS * 8), :]

    def far_out(regs, row, i):
        for t0 in (HALO, HALO + COLS // 2):
            outputs = range(t0, t0 + COLS // 2)
            filter_row(regs, fr, fs, row * COLS, range(COLS), out_ref, i * COLS - HALO, outputs)

    neighbour_rows(h_ref, parity_of("inline"), far_out)


def inverse_kernel(acc_ref, side_ref, mate_ref, tab_ref, out_ref, work):
    odd = parity_of("xline")
    keep = keep_of("xline")
    work[...] = acc_ref[...]
    for i in range(ROWS):
        source = pl.ds(i * HALO * 8, HALO * 8)
        side = pl.ds(pl.multiple_of((i * COLS + 12 * odd) * 8, 8), HALO * 8)
        work[side, :] = work[side, :] + side_ref[source, :] * keep
        mate = pl.ds(pl.multiple_of((i * COLS + 12 - 12 * odd) * 8, 8), HALO * 8)
        work[mate, :] = work[mate, :] + mate_ref[source, :]
    lane = lax.broadcasted_iota(jnp.int32, (ROWS * COLS, 128), 1)
    parts = []
    for parity in (0, 1):
        tiles = [work[pl.ds(s, ROWS * COLS, stride=8), :] for s in SUBLANE[parity]]
        if parity == 0:
            tiles[0] = jnp.where(lane == 0, 0.5 * tiles[0], tiles[0])
        spectrum = jnp.concatenate(tiles, axis=1)
        parts.append(dot3(spectrum, tab_ref[2 * parity], tab_ref[2 * parity + 1]) * (2.0 / NT))
    out_ref[:, :, :HALF] = (parts[0] + parts[1]).reshape(ROWS, COLS, HALF)
    out_ref[:, :, HALF:] = (parts[0] - parts[1]).reshape(ROWS, COLS, HALF)


def call(kernel, outs, scratch, args, weight=0):
    return pl.pallas_call(
        kernel,
        out_shape=[jax.ShapeDtypeStruct(shape, jnp.float32) for shape in outs],
        scratch_shapes=[pltpu.VMEM(shape, jnp.float32) for shape in scratch],
        compiler_params=pltpu.CompilerParams(vmem_limit_bytes=40 * 2**20),
        cost_estimate=pl.CostEstimate(flops=weight * 10**9, bytes_accessed=0, transcendentals=0) if weight else None,
    )(*args)


def permutations(inline, xline):
    number = lambda i, j: i * xline + j
    side, far = [], []
    for i in range(inline):
        for j in range(xline):
            k = j - 1 if j % 2 == 0 else j + 1
            side.append((number(i, j), number(i, k) if 0 <= k < xline else number(i ^ 1, j)))
            k = i - 1 if i % 2 == 0 else i + 1
            far.append((number(i, j), number(k, j) if 0 <= k < inline else number(i, j ^ 1)))
    near = [(i, i ^ 1) for i in range(inline)]
    mate = [(j, j ^ 1) for j in range(xline)]
    return side, far, near, mate


def per_device(traces, filters):
    side, far, near, mate = permutations(lax.axis_size("inline"), lax.axis_size("xline"))
    tab, inverse_tab = (jnp.asarray(table) for table in tables())
    taps = jnp.transpose(filters.reshape(2, HALF // 128, 128, TAPS * TAPS), (3, 1, 0, 2)).reshape(-1, 128)

    rows = (HALO * COLS, NT)
    to_far, to_near = call(edges_kernel, [rows, rows], [], (traces,), weight=2)
    from_far = lax.ppermute(to_far, AXES, far)
    from_near = lax.ppermute(to_near, "inline", near)

    wide = (ROWS * WIDE * 8, 128)
    frame = (ROWS * COLS * 8, 128)
    spot = (ROWS * HALO * 8, 128)
    rows_frame = (HALO * COLS * 8, 128)
    (h,) = call(taps_kernel, [(2 * TAPS * TAPS * 8, 128)], [], (taps,), weight=1)
    (acc,) = call(own_kernel, [wide], [frame, frame], (traces, tab, h), weight=10)
    (acc,) = call(near_kernel, [wide], [rows_frame] * 2, (acc, from_near, tab, h), weight=2)
    to_side, to_mate, fr, fs = call(ends_kernel, [spot, spot, rows_frame, rows_frame], [], (acc, from_far, tab, h))
    from_mate = lax.ppermute(to_mate, "xline", mate)
    from_side = lax.ppermute(to_side, AXES, side)
    (acc,) = call(inner_kernel, [frame], [], (acc, fr, fs, h), weight=2)
    (out,) = call(inverse_kernel, [(ROWS, COLS, NT)], [frame], (acc, from_side, from_mate, inverse_tab))
    return out


def solution(mesh):
    return jax.shard_map(
        per_device,
        mesh=mesh,
        in_specs=(P("inline", "xline", None), P()),
        out_specs=P("inline", "xline", None),
        check_vma=False,
    )
```

```python
import math

import jax
import jax.numpy as jnp
import ml_dtypes
import numpy as np
from jax import lax
from jax.experimental import pallas as pl
from jax.experimental.pallas import tpu as pltpu
from jax.sharding import PartitionSpec as P

ROWS, COLS, NT = 8, 16, 1024
HALF = NT // 2
HALO = 4
TAPS = 9
WIDE = COLS + 2 * HALO
REST = COLS - HALO
AXES = ("inline", "xline")
AHEAD = (4, 5, 2, 0)


def split_bf16(table):
    high = table.astype(ml_dtypes.bfloat16)
    low = (table - high.astype(np.float64)).astype(ml_dtypes.bfloat16)
    return high, low


def tables():
    time_index = np.arange(HALF)[:, None]
    out, transposed = [], []
    for parity in (0, 1):
        bins = 2 * np.arange(HALF // 2)[None, :] + parity
        phase = (time_index * bins % NT) * (2.0 * math.pi / NT)
        table = np.concatenate([np.cos(phase), -np.sin(phase)], axis=1)
        out.extend(split_bf16(table))
        transposed.extend(split_bf16(table.T))
    return np.stack(out), np.stack(transposed)


SUBLANE = ((0, 1, 4, 5), (2, 3, 6, 7))


def dot(a, b):
    return lax.dot_general(a, b, (((1,), (0,)), ((), ())), preferred_element_type=jnp.float32)


def high_low(x):
    high = x.astype(jnp.bfloat16)
    return high, (x - high.astype(jnp.float32)).astype(jnp.bfloat16)


def dot3(x, high, low):
    xh, xl = high_low(x)
    return dot(xh, high) + (dot(xl, high) + dot(xh, low))


def forward(x, tab_ref):
    first, second = x[:, :HALF], x[:, HALF:]
    tiles = [None] * 8
    for parity, value in ((0, first + second), (1, first - second)):
        product = dot3(value, tab_ref[2 * parity], tab_ref[2 * parity + 1])
        for c in range(4):
            tiles[SUBLANE[parity][c]] = product[:, c * 128 : (c + 1) * 128]
    return tiles


def place(tiles, start, count, ref, swapped_ref, base):
    for s in range(8):
        value = tiles[s][start : start + count]
        ref[pl.ds(base * 8 + s, count, stride=8), :] = value
        swapped_ref[pl.ds(base * 8 + (s ^ 4), count, stride=8), :] = value


def filter_row(regs, ref, swapped_ref, in_base, inputs, acc_ref, out_base, outputs):
    spot = lambda base, n: pl.ds((base + n) * 8, 8)
    reach = lambda t: any(n <= t <= n + 2 * HALO for n in inputs)
    acc = {t: acc_ref[spot(out_base, t), :] for t in outputs if reach(t)}
    for n in inputs:
        pairs = [(n - b + 2 * HALO, b) for b in range(TAPS) if n - b + 2 * HALO in acc]
        if pairs:
            x, xs = ref[spot(in_base, n), :], swapped_ref[spot(in_base, n), :]
            for t, b in pairs:
                acc[t] = acc[t] + (regs[b] * x + regs[TAPS + b] * xs)
    for t in acc:
        acc_ref[spot(out_base, t), :] = acc[t]


def load_taps(h_ref, a):
    tap = lambda b, part: h_ref[pl.ds(((a * TAPS + b) * 2 + part) * 8, 8), :]
    return [tap(b, 0) for b in range(TAPS)] + [tap(b, 1) for b in range(TAPS)]


def parity_of(axis):
    return lax.rem(lax.axis_index(axis), 2)


def keep_of(axis):
    index = lax.axis_index(axis)
    is_end = (index == 0) | (index == lax.axis_size(axis) - 1)
    return jnp.where(is_end, 0.0, 1.0).astype(jnp.float32)


def each_parity(body):
    odd = parity_of("xline")
    for parity in (0, 1):
        pl.when(odd == parity)(lambda: body(parity))


def side_columns(parity):
    return range(COLS - HALO, COLS) if parity else range(HALO)


def other_columns(parity):
    return range(COLS - HALO) if parity else range(HALO, COLS)


def edges_kernel(x_ref, far_side, near_side, far_rest, near_rest):
    odd_row = parity_of("inline")

    def body(parity):
        side, rest = side_columns(parity), other_columns(parity)
        for first, side_ref, rest_ref in (
            (HALO * odd_row, far_side, far_rest),
            (HALO - HALO * odd_row, near_side, near_rest),
        ):
            for r in range(HALO):
                row = first + r
                side_ref[r * HALO : (r + 1) * HALO, :] = x_ref[row, side[0] : side[-1] + 1, :]
                rest_ref[r * REST : (r + 1) * REST, :] = x_ref[row, rest[0] : rest[-1] + 1, :]

    each_parity(body)


def taps_kernel(f_ref, h_ref):
    source = lax.broadcasted_iota(jnp.int32, (HALF, HALF), 0)
    target = lax.broadcasted_iota(jnp.int32, (HALF, HALF), 1)
    wanted = jnp.where(target < HALF // 2, 2 * target, 2 * target - (HALF - 1))
    order = jnp.where(source == wanted, 1.0, 0.0).astype(jnp.bfloat16)
    count = TAPS * TAPS
    for part in (0, 1):
        rest = jnp.concatenate([f_ref[pl.ds(2 * tile + part, count, stride=8), :] for tile in range(4)], axis=1)
        taps = 0.0
        for _ in range(3):
            piece = rest.astype(jnp.bfloat16)
            rest = rest - piece.astype(jnp.float32)
            taps = taps + dot(piece, order)
        for s in range(4):
            value = taps[:, s * 128 : (s + 1) * 128]
            h_ref[pl.ds(part * 8 + s, count, stride=16), :] = -value if part else value
            h_ref[pl.ds(part * 8 + s + 4, count, stride=16), :] = value


def neighbour_rows(h_ref, below, body):
    for step in range(HALO):
        regs = load_taps(h_ref, step + (HALO + 1) * below)

        def out_row(i, carry):
            body(regs, i + step - 7 * below, i)
            return carry

        first = (ROWS - 1 - step) * below
        lax.fori_loop(first, HALO - step + (HALO + step) * below, out_row, 0)


def own_rows(h_ref, body, first=0, last=TAPS):
    def tap_row(a, carry):
        regs = load_taps(h_ref, a)

        def out_row(i, carry):
            body(regs, i + a - HALO, i)
            return carry

        return lax.fori_loop(jnp.maximum(0, HALO - a), jnp.minimum(ROWS, ROWS + HALO - a), out_row, carry)

    lax.fori_loop(first, last, tap_row, 0)


def side_outputs(parity):
    return range(COLS + HALO, WIDE) if parity else range(HALO)


def spectra_kernel(x_ref, tab_ref, h_ref, fr, fs, side_ref):
    place(forward(x_ref[...].reshape(ROWS * COLS, NT), tab_ref), 0, ROWS * COLS, fr, fs, 0)
    side_ref[...] = jnp.zeros_like(side_ref)

    def body(parity):
        inputs, outputs = side_columns(parity), side_outputs(parity)

        def out(regs, row, i):
            filter_row(regs, fr, fs, row * COLS, inputs, side_ref, i * HALO - outputs[0], outputs)

        own_rows(h_ref, out)

    each_parity(body)


def side_kernel(own_ref, near_ref, far_ref, tab_ref, h_ref, acc_ref, side_ref, nr, ns, fr, fs):
    keep = keep_of("inline")
    tiles = forward(jnp.concatenate([near_ref[...], far_ref[...]], axis=0), tab_ref)
    count = HALO * HALO
    place(tiles, 0, count, nr, ns, 0)
    place([tile * keep for tile in tiles], count, count, fr, fs, 0)
    side_ref[...] = own_ref[...]
    far_below = parity_of("inline")

    def body(parity):
        inputs, outputs = side_columns(parity), side_outputs(parity)
        for ref, swapped_ref, below in ((nr, ns, 1 - far_below), (fr, fs, far_below)):

            def out(regs, row, i):
                base = row * HALO - inputs[0]
                filter_row(regs, ref, swapped_ref, base, inputs, side_ref, i * HALO - outputs[0], outputs)

            neighbour_rows(h_ref, below, out)

    each_parity(body)


def halves(outputs):
    middle = len(outputs) // 2
    return outputs[:middle], outputs[middle:]


def inner_outputs(parity):
    return range(COLS + HALO) if parity else range(HALO, WIDE)


def ahead():
    place_in_run = lax.rem(lax.axis_index("xline"), 8)
    count = jnp.where((place_in_run == 1) | (place_in_run == 3), AHEAD[1], AHEAD[3])
    count = jnp.where(place_in_run == 0, AHEAD[0], count)
    return jnp.where(place_in_run == 5, AHEAD[2], count)


def filter_own(fr, fs, h_ref, acc_ref, first, last):
    def body(parity):
        def out(regs, row, i):
            for outputs in halves(inner_outputs(parity)):
                filter_row(regs, fr, fs, row * COLS, range(COLS), acc_ref, i * WIDE, outputs)

        own_rows(h_ref, out, first, last)

    each_parity(body)


def early_kernel(fr, fs, h_ref, acc_ref):
    acc_ref[...] = jnp.zeros_like(acc_ref)
    filter_own(fr, fs, h_ref, acc_ref, 0, ahead())


def late_kernel(acc_in, fr, fs, h_ref, acc_ref):
    acc_ref[...] = acc_in[...]
    filter_own(fr, fs, h_ref, acc_ref, ahead(), TAPS)


def near_kernel(acc_in, rest_ref, nr, ns, tab_ref, h_ref, acc_ref, fr, fs):
    acc_ref[...] = acc_in[...]
    place(forward(rest_ref[...], tab_ref), 0, HALO * REST, fr, fs, 0)

    def body(parity):
        side, rest = side_columns(parity), other_columns(parity)

        def out(regs, row, i):
            for outputs in halves(inner_outputs(parity)):
                filter_row(regs, nr, ns, row * HALO - side[0], side, acc_ref, i * WIDE, outputs)
                filter_row(regs, fr, fs, row * REST - rest[0], rest, acc_ref, i * WIDE, outputs)

        neighbour_rows(h_ref, 1 - parity_of("inline"), out)

    each_parity(body)


def mate_kernel(acc_ref, rest_ref, tab_ref, h_ref, mate_ref, fr, fs):
    keep = keep_of("inline")
    place([tile * keep for tile in forward(rest_ref[...], tab_ref)], 0, HALO * REST, fr, fs, 0)

    def body(parity):
        outputs, rest = side_outputs(1 - parity), other_columns(parity)
        inputs = side_columns(1 - parity)
        for i in range(ROWS):
            source = pl.ds((i * WIDE + outputs[0]) * 8, HALO * 8)
            mate_ref[pl.ds(i * HALO * 8, HALO * 8), :] = acc_ref[source, :]

        def out(regs, row, i):
            filter_row(regs, fr, fs, row * REST - rest[0], inputs, mate_ref, i * HALO - outputs[0], outputs)

        neighbour_rows(h_ref, parity_of("inline"), out)

    each_parity(body)


def inner_kernel(acc_ref, rr, rs, sr, ss, h_ref, out_ref):
    def body(parity):
        side, rest = side_columns(parity), other_columns(parity)
        for i in range(ROWS):
            out_ref[pl.ds(i * COLS * 8, COLS * 8), :] = acc_ref[pl.ds((i * WIDE + HALO) * 8, COLS * 8), :]

        def out(regs, row, i):
            for outputs in halves(range(HALO, HALO + COLS)):
                filter_row(regs, sr, ss, row * HALO - side[0], side, out_ref, i * COLS - HALO, outputs)
                filter_row(regs, rr, rs, row * REST - rest[0], rest, out_ref, i * COLS - HALO, outputs)

        neighbour_rows(h_ref, parity_of("inline"), out)

    each_parity(body)


def add_kernel(acc_ref, side_ref, out_ref):
    odd, keep = parity_of("xline"), keep_of("xline")
    out_ref[...] = acc_ref[...]
    for i in range(ROWS):
        target = pl.ds(pl.multiple_of((i * COLS + 12 * odd) * 8, 8), HALO * 8)
        out_ref[target, :] = out_ref[target, :] + side_ref[pl.ds(i * HALO * 8, HALO * 8), :] * keep


def inverse_kernel(acc_ref, mate_ref, tab_ref, out_ref, work):
    odd = parity_of("xline")
    work[...] = acc_ref[...]
    for i in range(ROWS):
        source = pl.ds(i * HALO * 8, HALO * 8)
        mate = pl.ds(pl.multiple_of((i * COLS + 12 - 12 * odd) * 8, 8), HALO * 8)
        work[mate, :] = work[mate, :] + mate_ref[source, :]
    lane = lax.broadcasted_iota(jnp.int32, (ROWS * COLS, 128), 1)
    parts = []
    for parity in (0, 1):
        tiles = [work[pl.ds(s, ROWS * COLS, stride=8), :] for s in SUBLANE[parity]]
        if parity == 0:
            tiles[0] = jnp.where(lane == 0, 0.5 * tiles[0], tiles[0])
        spectrum = jnp.concatenate(tiles, axis=1)
        parts.append(dot3(spectrum, tab_ref[2 * parity], tab_ref[2 * parity + 1]) * (2.0 / NT))
    out_ref[:, :, :HALF] = (parts[0] + parts[1]).reshape(ROWS, COLS, HALF)
    out_ref[:, :, HALF:] = (parts[0] - parts[1]).reshape(ROWS, COLS, HALF)


def call(kernel, outs, scratch, args, specs=None, weight=0):
    return pl.pallas_call(
        kernel,
        out_shape=[jax.ShapeDtypeStruct(shape, jnp.float32) for shape in outs],
        in_specs=specs or [pl.BlockSpec()] * len(args),
        scratch_shapes=[pltpu.VMEM(shape, jnp.float32) for shape in scratch],
        compiler_params=pltpu.CompilerParams(vmem_limit_bytes=40 * 2**20),
        cost_estimate=pl.CostEstimate(flops=weight * 10**9, bytes_accessed=0, transcendentals=0) if weight else None,
    )(*args)


def permutations(inline, xline):
    number = lambda i, j: i * xline + j
    side, far = [], []
    for i in range(inline):
        for j in range(xline):
            k = j - 1 if j % 2 == 0 else j + 1
            side.append((number(i, j), number(i, k) if 0 <= k < xline else number(i ^ 1, j)))
            k = i - 1 if i % 2 == 0 else i + 1
            far.append((number(i, j), number(k, j) if 0 <= k < inline else number(i, j ^ 1)))
    near = [(i, i ^ 1) for i in range(inline)]
    mate = [(j, j ^ 1) for j in range(xline)]
    return side, far, near, mate


def per_device(traces, filters):
    side, far, near, mate = permutations(lax.axis_size("inline"), lax.axis_size("xline"))
    tab, inverse_tab = (jnp.asarray(table) for table in tables())
    taps = jnp.transpose(filters.reshape(2, HALF // 128, 128, TAPS * TAPS), (3, 1, 0, 2)).reshape(-1, 128)

    corner, rest = (HALO * HALO, NT), (HALO * REST, NT)
    far_side, near_side, far_rest, near_rest = call(edges_kernel, [corner, corner, rest, rest], [], (traces,), weight=2)
    far_side = lax.ppermute(far_side, AXES, far)
    near_side = lax.ppermute(near_side, "inline", near)
    far_rest = lax.ppermute(far_rest, AXES, far)
    near_rest = lax.ppermute(near_rest, "inline", near)

    wide = (ROWS * WIDE * 8, 128)
    frame = (ROWS * COLS * 8, 128)
    spot = (ROWS * HALO * 8, 128)
    side_frame = (HALO * HALO * 8, 128)
    rest_frame = (HALO * REST * 8, 128)
    (h,) = call(taps_kernel, [(2 * TAPS * TAPS * 8, 128)], [], (taps,))
    fr, fs, to_side = call(spectra_kernel, [frame, frame, spot], [], (traces, tab, h))
    (acc,) = call(early_kernel, [wide], [], (fr, fs, h))
    vmem, anywhere = pl.BlockSpec(memory_space=pltpu.VMEM), pl.BlockSpec(memory_space=pl.ANY)
    to_side, nr, ns, sr, ss = call(
        side_kernel,
        [spot] + [side_frame] * 4,
        [],
        (to_side, near_side, far_side, tab, h, acc),
        specs=[vmem] * 5 + [anywhere],
    )
    from_side = lax.ppermute(to_side, AXES, side)
    (acc,) = call(late_kernel, [wide], [], (acc, fr, fs, h), weight=20)
    (acc,) = call(near_kernel, [wide], [rest_frame] * 2, (acc, near_rest, nr, ns, tab, h))
    to_mate, rr, rs = call(mate_kernel, [spot, rest_frame, rest_frame], [], (acc, far_rest, tab, h))
    from_mate = lax.ppermute(to_mate, "xline", mate)
    (acc,) = call(inner_kernel, [frame], [], (acc, rr, rs, sr, ss, h), weight=1)
    (acc,) = call(add_kernel, [frame], [], (acc, from_side), weight=5)
    (out,) = call(inverse_kernel, [(ROWS, COLS, NT)], [frame], (acc, from_mate, inverse_tab))
    return out


def solution(mesh):
    return jax.shard_map(
        per_device,
        mesh=mesh,
        in_specs=(P("inline", "xline", None), P()),
        out_specs=P("inline", "xline", None),
        check_vma=False,
    )
```

```python
import math

import jax
import jax.numpy as jnp
import ml_dtypes
import numpy as np
from jax import lax
from jax.experimental import pallas as pl
from jax.experimental.pallas import tpu as pltpu
from jax.sharding import PartitionSpec as P

ROWS, COLS, NT = 8, 16, 1024
HALF = NT // 2
HALO = 4
TAPS = 9
WIDE = COLS + 2 * HALO
REST = COLS - HALO
AXES = ("inline", "xline")
AHEAD = (4, 5, 2, 0)


def split_bf16(table):
    high = table.astype(ml_dtypes.bfloat16)
    low = (table - high.astype(np.float64)).astype(ml_dtypes.bfloat16)
    return high, low


def tables():
    time_index = np.arange(HALF)[:, None]
    out, transposed = [], []
    for parity in (0, 1):
        bins = 2 * np.arange(HALF // 2)[None, :] + parity
        phase = (time_index * bins % NT) * (2.0 * math.pi / NT)
        table = np.concatenate([np.cos(phase), -np.sin(phase)], axis=1)
        out.extend(split_bf16(table))
        transposed.extend(split_bf16(table.T))
    return np.stack(out + transposed)


SUBLANE = ((0, 1, 4, 5), (2, 3, 6, 7))


def dot(a, b):
    return lax.dot_general(a, b, (((1,), (0,)), ((), ())), preferred_element_type=jnp.float32)


def high_low(x):
    high = x.astype(jnp.bfloat16)
    return high, (x - high.astype(jnp.float32)).astype(jnp.bfloat16)


def dot3(x, high, low):
    xh, xl = high_low(x)
    return dot(xh, high) + (dot(xl, high) + dot(xh, low))


def forward(x, tab_ref):
    first, second = x[:, :HALF], x[:, HALF:]
    tiles = [None] * 8
    for parity, value in ((0, first + second), (1, first - second)):
        product = dot3(value, tab_ref[2 * parity], tab_ref[2 * parity + 1])
        for c in range(4):
            tiles[SUBLANE[parity][c]] = product[:, c * 128 : (c + 1) * 128]
    return tiles


def place(tiles, start, count, ref, swapped_ref, base):
    for s in range(8):
        value = tiles[s][start : start + count]
        ref[pl.ds(base * 8 + s, count, stride=8), :] = value
        swapped_ref[pl.ds(base * 8 + (s ^ 4), count, stride=8), :] = value


def filter_row(regs, ref, swapped_ref, in_base, inputs, acc_ref, out_base, outputs):
    spot = lambda base, n: pl.ds((base + n) * 8, 8)
    reach = lambda t: any(n <= t <= n + 2 * HALO for n in inputs)
    acc = {t: acc_ref[spot(out_base, t), :] for t in outputs if reach(t)}
    for n in inputs:
        pairs = [(n - b + 2 * HALO, b) for b in range(TAPS) if n - b + 2 * HALO in acc]
        if pairs:
            x, xs = ref[spot(in_base, n), :], swapped_ref[spot(in_base, n), :]
            for t, b in pairs:
                acc[t] = acc[t] + (regs[b] * x + regs[TAPS + b] * xs)
    for t in acc:
        acc_ref[spot(out_base, t), :] = acc[t]


def load_taps(h_ref, a):
    tap = lambda b, part: h_ref[pl.ds(((a * TAPS + b) * 2 + part) * 8, 8), :]
    return [tap(b, 0) for b in range(TAPS)] + [tap(b, 1) for b in range(TAPS)]


def parity_of(axis):
    return lax.rem(lax.axis_index(axis), 2)


def keep_of(axis):
    index = lax.axis_index(axis)
    is_end = (index == 0) | (index == lax.axis_size(axis) - 1)
    return jnp.where(is_end, 0.0, 1.0).astype(jnp.float32)


def each_parity(body):
    odd = parity_of("xline")
    for parity in (0, 1):
        pl.when(odd == parity)(lambda: body(parity))


def side_columns(parity):
    return range(COLS - HALO, COLS) if parity else range(HALO)


def other_columns(parity):
    return range(COLS - HALO) if parity else range(HALO, COLS)


def edges_kernel(x_ref, far_side, far_rest, near_rows):
    odd_row = parity_of("inline")

    def body(parity):
        side, rest = side_columns(parity), other_columns(parity)
        for r in range(HALO):
            row = HALO * odd_row + r
            far_side[r * HALO : (r + 1) * HALO, :] = x_ref[row, side[0] : side[-1] + 1, :]
            far_rest[r * REST : (r + 1) * REST, :] = x_ref[row, rest[0] : rest[-1] + 1, :]

    each_parity(body)
    for r in range(HALO):
        near_rows[r * COLS : (r + 1) * COLS, :] = x_ref[HALO - HALO * odd_row + r]


def taps_kernel(f_ref, h_ref):
    source = lax.broadcasted_iota(jnp.int32, (HALF, HALF), 0)
    target = lax.broadcasted_iota(jnp.int32, (HALF, HALF), 1)
    wanted = jnp.where(target < HALF // 2, 2 * target, 2 * target - (HALF - 1))
    order = jnp.where(source == wanted, 1.0, 0.0).astype(jnp.bfloat16)
    count = TAPS * TAPS
    for part in (0, 1):
        rest = jnp.concatenate([f_ref[pl.ds(2 * tile + part, count, stride=8), :] for tile in range(4)], axis=1)
        taps = 0.0
        for _ in range(3):
            piece = rest.astype(jnp.bfloat16)
            rest = rest - piece.astype(jnp.float32)
            taps = taps + dot(piece, order)
        for s in range(4):
            value = taps[:, s * 128 : (s + 1) * 128]
            h_ref[pl.ds(part * 8 + s, count, stride=16), :] = -value if part else value
            h_ref[pl.ds(part * 8 + s + 4, count, stride=16), :] = value


def neighbour_rows(h_ref, below, body):
    for step in range(HALO):
        regs = load_taps(h_ref, step + (HALO + 1) * below)

        def out_row(i, carry):
            body(regs, i + step - 7 * below, i)
            return carry

        first = (ROWS - 1 - step) * below
        lax.fori_loop(first, HALO - step + (HALO + step) * below, out_row, 0)


def own_rows(h_ref, body, first=0, last=TAPS):
    def tap_row(a, carry):
        regs = load_taps(h_ref, a)

        def out_row(i, carry):
            body(regs, i + a - HALO, i)
            return carry

        return lax.fori_loop(jnp.maximum(0, HALO - a), jnp.minimum(ROWS, ROWS + HALO - a), out_row, carry)

    lax.fori_loop(first, last, tap_row, 0)


def side_outputs(parity):
    return range(COLS + HALO, WIDE) if parity else range(HALO)


def spectra_kernel(x_ref, tab_ref, h_ref, fr, fs, side_ref):
    place(forward(x_ref[...].reshape(ROWS * COLS, NT), tab_ref), 0, ROWS * COLS, fr, fs, 0)
    side_ref[...] = jnp.zeros_like(side_ref)

    def body(parity):
        inputs, outputs = side_columns(parity), side_outputs(parity)

        def out(regs, row, i):
            filter_row(regs, fr, fs, row * COLS, inputs, side_ref, i * HALO - outputs[0], outputs)

        own_rows(h_ref, out)

    each_parity(body)


def side_kernel(own_ref, near_ref, far_ref, tab_ref, h_ref, acc_ref, side_ref, nr, ns, fr, fs):
    keep = keep_of("inline")
    tiles = forward(jnp.concatenate([near_ref[...], far_ref[...]], axis=0), tab_ref)
    place(tiles, 0, HALO * COLS, nr, ns, 0)
    place([tile * keep for tile in tiles], HALO * COLS, HALO * HALO, fr, fs, 0)
    side_ref[...] = own_ref[...]
    far_below = parity_of("inline")

    def body(parity):
        inputs, outputs = side_columns(parity), side_outputs(parity)

        def near_out(regs, row, i):
            filter_row(regs, nr, ns, row * COLS, inputs, side_ref, i * HALO - outputs[0], outputs)

        def far_out(regs, row, i):
            base = row * HALO - inputs[0]
            filter_row(regs, fr, fs, base, inputs, side_ref, i * HALO - outputs[0], outputs)

        neighbour_rows(h_ref, 1 - far_below, near_out)
        neighbour_rows(h_ref, far_below, far_out)

    each_parity(body)


def halves(outputs):
    middle = len(outputs) // 2
    return outputs[:middle], outputs[middle:]


def inner_outputs(parity):
    return range(COLS + HALO) if parity else range(HALO, WIDE)


def ahead():
    place_in_run = lax.rem(lax.axis_index("xline"), 8)
    count = jnp.where((place_in_run == 1) | (place_in_run == 3), AHEAD[1], AHEAD[3])
    count = jnp.where(place_in_run == 0, AHEAD[0], count)
    return jnp.where(place_in_run == 5, AHEAD[2], count)


def filter_own(fr, fs, h_ref, acc_ref, first, last):
    def body(parity):
        def out(regs, row, i):
            for outputs in halves(inner_outputs(parity)):
                filter_row(regs, fr, fs, row * COLS, range(COLS), acc_ref, i * WIDE, outputs)

        own_rows(h_ref, out, first, last)

    each_parity(body)


def early_kernel(fr, fs, h_ref, acc_ref):
    acc_ref[...] = jnp.zeros_like(acc_ref)
    filter_own(fr, fs, h_ref, acc_ref, 0, ahead())


def late_kernel(acc_in, fr, fs, h_ref, acc_ref):
    acc_ref[...] = acc_in[...]
    filter_own(fr, fs, h_ref, acc_ref, ahead(), TAPS)


def near_kernel(acc_in, nr, ns, h_ref, acc_ref):
    acc_ref[...] = acc_in[...]

    def body(parity):
        def out(regs, row, i):
            for outputs in halves(inner_outputs(parity)):
                filter_row(regs, nr, ns, row * COLS, range(COLS), acc_ref, i * WIDE, outputs)

        neighbour_rows(h_ref, 1 - parity_of("inline"), out)

    each_parity(body)


def mate_kernel(acc_ref, rest_ref, tab_ref, h_ref, mate_ref, fr, fs):
    keep = keep_of("inline")
    place([tile * keep for tile in forward(rest_ref[...], tab_ref)], 0, HALO * REST, fr, fs, 0)

    def body(parity):
        outputs, rest = side_outputs(1 - parity), other_columns(parity)
        inputs = side_columns(1 - parity)
        for i in range(ROWS):
            source = pl.ds((i * WIDE + outputs[0]) * 8, HALO * 8)
            mate_ref[pl.ds(i * HALO * 8, HALO * 8), :] = acc_ref[source, :]

        def out(regs, row, i):
            filter_row(regs, fr, fs, row * REST - rest[0], inputs, mate_ref, i * HALO - outputs[0], outputs)

        neighbour_rows(h_ref, parity_of("inline"), out)

    each_parity(body)


def inner_kernel(acc_ref, rr, rs, sr, ss, h_ref, out_ref):
    def body(parity):
        side, rest = side_columns(parity), other_columns(parity)
        for i in range(ROWS):
            out_ref[pl.ds(i * COLS * 8, COLS * 8), :] = acc_ref[pl.ds((i * WIDE + HALO) * 8, COLS * 8), :]

        def out(regs, row, i):
            for outputs in halves(range(HALO, HALO + COLS)):
                filter_row(regs, sr, ss, row * HALO - side[0], side, out_ref, i * COLS - HALO, outputs)
                filter_row(regs, rr, rs, row * REST - rest[0], rest, out_ref, i * COLS - HALO, outputs)

        neighbour_rows(h_ref, parity_of("inline"), out)

    each_parity(body)


def add_kernel(acc_ref, side_ref, out_ref):
    odd, keep = parity_of("xline"), keep_of("xline")
    out_ref[...] = acc_ref[...]
    for i in range(ROWS):
        target = pl.ds(pl.multiple_of((i * COLS + 12 * odd) * 8, 8), HALO * 8)
        out_ref[target, :] = out_ref[target, :] + side_ref[pl.ds(i * HALO * 8, HALO * 8), :] * keep


def inverse_kernel(acc_ref, mate_ref, tab_ref, out_ref, work):
    odd = parity_of("xline")
    work[...] = acc_ref[...]
    for i in range(ROWS):
        source = pl.ds(i * HALO * 8, HALO * 8)
        mate = pl.ds(pl.multiple_of((i * COLS + 12 - 12 * odd) * 8, 8), HALO * 8)
        work[mate, :] = work[mate, :] + mate_ref[source, :]
    lane = lax.broadcasted_iota(jnp.int32, (ROWS * COLS, 128), 1)
    parts = []
    for parity in (0, 1):
        tiles = [work[pl.ds(s, ROWS * COLS, stride=8), :] for s in SUBLANE[parity]]
        if parity == 0:
            tiles[0] = jnp.where(lane == 0, 0.5 * tiles[0], tiles[0])
        spectrum = jnp.concatenate(tiles, axis=1)
        parts.append(dot3(spectrum, tab_ref[4 + 2 * parity], tab_ref[5 + 2 * parity]) * (2.0 / NT))
    out_ref[:, :, :HALF] = (parts[0] + parts[1]).reshape(ROWS, COLS, HALF)
    out_ref[:, :, HALF:] = (parts[0] - parts[1]).reshape(ROWS, COLS, HALF)


def call(kernel, outs, scratch, args, specs=None, weight=0):
    return pl.pallas_call(
        kernel,
        out_shape=[jax.ShapeDtypeStruct(shape, jnp.float32) for shape in outs],
        in_specs=specs or [pl.BlockSpec()] * len(args),
        scratch_shapes=[pltpu.VMEM(shape, jnp.float32) for shape in scratch],
        compiler_params=pltpu.CompilerParams(vmem_limit_bytes=40 * 2**20),
        cost_estimate=pl.CostEstimate(flops=weight * 10**9, bytes_accessed=0, transcendentals=0) if weight else None,
    )(*args)


def permutations(inline, xline):
    number = lambda i, j: i * xline + j
    side, far = [], []
    for i in range(inline):
        for j in range(xline):
            k = j - 1 if j % 2 == 0 else j + 1
            side.append((number(i, j), number(i, k) if 0 <= k < xline else number(i ^ 1, j)))
            k = i - 1 if i % 2 == 0 else i + 1
            far.append((number(i, j), number(k, j) if 0 <= k < inline else number(i, j ^ 1)))
    near = [(i, i ^ 1) for i in range(inline)]
    mate = [(j, j ^ 1) for j in range(xline)]
    return side, far, near, mate


def per_device(traces, filters):
    side, far, near, mate = permutations(lax.axis_size("inline"), lax.axis_size("xline"))
    tab = jnp.asarray(tables())
    taps = jnp.transpose(filters.reshape(2, HALF // 128, 128, TAPS * TAPS), (3, 1, 0, 2)).reshape(-1, 128)

    corner, rest, rows = ((HALO * columns, NT) for columns in (HALO, REST, COLS))
    far_side, far_rest, near_rows = call(edges_kernel, [corner, rest, rows], [], (traces,), weight=2)
    far_side = lax.ppermute(far_side, AXES, far)
    near_rows = lax.ppermute(near_rows, "inline", near)
    far_rest = lax.ppermute(far_rest, AXES, far)

    wide = (ROWS * WIDE * 8, 128)
    frame = (ROWS * COLS * 8, 128)
    spot = (ROWS * HALO * 8, 128)
    side_frame = (HALO * HALO * 8, 128)
    rest_frame = (HALO * REST * 8, 128)
    rows_frame = (HALO * COLS * 8, 128)
    (h,) = call(taps_kernel, [(2 * TAPS * TAPS * 8, 128)], [], (taps,))
    fr, fs, to_side = call(spectra_kernel, [frame, frame, spot], [], (traces, tab, h))
    (acc,) = call(early_kernel, [wide], [], (fr, fs, h))
    vmem, anywhere = pl.BlockSpec(memory_space=pltpu.VMEM), pl.BlockSpec(memory_space=pl.ANY)
    to_side, nr, ns, sr, ss = call(
        side_kernel,
        [spot] + [rows_frame] * 2 + [side_frame] * 2,
        [],
        (to_side, near_rows, far_side, tab, h, acc),
        specs=[vmem] * 5 + [anywhere],
    )
    from_side = lax.ppermute(to_side, AXES, side)
    (acc,) = call(late_kernel, [wide], [], (acc, fr, fs, h), weight=20)
    (acc,) = call(near_kernel, [wide], [], (acc, nr, ns, h))
    to_mate, rr, rs = call(mate_kernel, [spot, rest_frame, rest_frame], [], (acc, far_rest, tab, h))
    from_mate = lax.ppermute(to_mate, "xline", mate)
    (acc,) = call(inner_kernel, [frame], [], (acc, rr, rs, sr, ss, h), weight=1)
    (acc,) = call(add_kernel, [frame], [], (acc, from_side), weight=1)
    (out,) = call(inverse_kernel, [(ROWS, COLS, NT)], [frame], (acc, from_mate, tab))
    return out


def solution(mesh):
    return jax.shard_map(
        per_device,
        mesh=mesh,
        in_specs=(P("inline", "xline", None), P()),
        out_specs=P("inline", "xline", None),
        check_vma=False,
    )
```

```python
import math

import jax
import jax.numpy as jnp
import ml_dtypes
import numpy as np
from jax import lax
from jax.experimental import pallas as pl
from jax.experimental.pallas import tpu as pltpu
from jax.sharding import PartitionSpec as P

ROWS, COLS, NT = 8, 16, 1024
HALF = NT // 2
HALO = 4
TAPS = 9
WIDE = COLS + 2 * HALO
REST = COLS - HALO
AXES = ("inline", "xline")
AHEAD = (4, 5, 2, 0)


def split_bf16(table):
    high = table.astype(ml_dtypes.bfloat16)
    low = (table - high.astype(np.float64)).astype(ml_dtypes.bfloat16)
    return high, low


def tables():
    time_index = np.arange(HALF)[:, None]
    out, transposed = [], []
    for parity in (0, 1):
        bins = 2 * np.arange(HALF // 2)[None, :] + parity
        phase = (time_index * bins % NT) * (2.0 * math.pi / NT)
        table = np.concatenate([np.cos(phase), -np.sin(phase)], axis=1)
        out.extend(split_bf16(table))
        transposed.extend(split_bf16(table.T))
    return np.stack(out), np.stack(transposed)


SUBLANE = ((0, 1, 4, 5), (2, 3, 6, 7))


def dot(a, b):
    return lax.dot_general(a, b, (((1,), (0,)), ((), ())), preferred_element_type=jnp.float32)


def high_low(x):
    high = x.astype(jnp.bfloat16)
    return high, (x - high.astype(jnp.float32)).astype(jnp.bfloat16)


def dot3(x, high, low):
    xh, xl = high_low(x)
    return dot(xh, high) + (dot(xl, high) + dot(xh, low))


def forward(x, tab_ref):
    first, second = x[:, :HALF], x[:, HALF:]
    tiles = [None] * 8
    for parity, value in ((0, first + second), (1, first - second)):
        product = dot3(value, tab_ref[2 * parity], tab_ref[2 * parity + 1])
        for c in range(4):
            tiles[SUBLANE[parity][c]] = product[:, c * 128 : (c + 1) * 128]
    return tiles


def place(tiles, start, count, ref, swapped_ref, base):
    for s in range(8):
        value = tiles[s][start : start + count]
        ref[pl.ds(base * 8 + s, count, stride=8), :] = value
        swapped_ref[pl.ds(base * 8 + (s ^ 4), count, stride=8), :] = value


def filter_row(regs, ref, swapped_ref, in_base, inputs, acc_ref, out_base, outputs):
    spot = lambda base, n: pl.ds((base + n) * 8, 8)
    reach = lambda t: any(n <= t <= n + 2 * HALO for n in inputs)
    acc = {t: acc_ref[spot(out_base, t), :] for t in outputs if reach(t)}
    for n in inputs:
        pairs = [(n - b + 2 * HALO, b) for b in range(TAPS) if n - b + 2 * HALO in acc]
        if pairs:
            x, xs = ref[spot(in_base, n), :], swapped_ref[spot(in_base, n), :]
            for t, b in pairs:
                acc[t] = acc[t] + (regs[b] * x + regs[TAPS + b] * xs)
    for t in acc:
        acc_ref[spot(out_base, t), :] = acc[t]


def load_taps(h_ref, a):
    tap = lambda b, part: h_ref[pl.ds(((a * TAPS + b) * 2 + part) * 8, 8), :]
    return [tap(b, 0) for b in range(TAPS)] + [tap(b, 1) for b in range(TAPS)]


def parity_of(axis):
    return lax.rem(lax.axis_index(axis), 2)


def keep_of(axis):
    index = lax.axis_index(axis)
    is_end = (index == 0) | (index == lax.axis_size(axis) - 1)
    return jnp.where(is_end, 0.0, 1.0).astype(jnp.float32)


def each_parity(body):
    odd = parity_of("xline")
    for parity in (0, 1):
        pl.when(odd == parity)(lambda: body(parity))


def side_columns(parity):
    return range(COLS - HALO, COLS) if parity else range(HALO)


def other_columns(parity):
    return range(COLS - HALO) if parity else range(HALO, COLS)


def edges_kernel(x_ref, far_side, far_rest, near_rows):
    odd_row = parity_of("inline")

    def body(parity):
        side, rest = side_columns(parity), other_columns(parity)
        for r in range(HALO):
            row = HALO * odd_row + r
            far_side[r * HALO : (r + 1) * HALO, :] = x_ref[row, side[0] : side[-1] + 1, :]
            far_rest[r * REST : (r + 1) * REST, :] = x_ref[row, rest[0] : rest[-1] + 1, :]

    each_parity(body)
    for r in range(HALO):
        near_rows[r * COLS : (r + 1) * COLS, :] = x_ref[HALO - HALO * odd_row + r]


def taps_kernel(f_ref, h_ref):
    source = lax.broadcasted_iota(jnp.int32, (HALF, HALF), 0)
    target = lax.broadcasted_iota(jnp.int32, (HALF, HALF), 1)
    wanted = jnp.where(target < HALF // 2, 2 * target, 2 * target - (HALF - 1))
    order = jnp.where(source == wanted, 1.0, 0.0).astype(jnp.bfloat16)
    count = TAPS * TAPS
    for part in (0, 1):
        rest = jnp.concatenate([f_ref[pl.ds(2 * tile + part, count, stride=8), :] for tile in range(4)], axis=1)
        taps = 0.0
        for _ in range(3):
            piece = rest.astype(jnp.bfloat16)
            rest = rest - piece.astype(jnp.float32)
            taps = taps + dot(piece, order)
        for s in range(4):
            value = taps[:, s * 128 : (s + 1) * 128]
            h_ref[pl.ds(part * 8 + s, count, stride=16), :] = -value if part else value
            h_ref[pl.ds(part * 8 + s + 4, count, stride=16), :] = value


def neighbour_rows(h_ref, below, body):
    for step in range(HALO):
        regs = load_taps(h_ref, step + (HALO + 1) * below)

        def out_row(i, carry):
            body(regs, i + step - 7 * below, i)
            return carry

        first = (ROWS - 1 - step) * below
        lax.fori_loop(first, HALO - step + (HALO + step) * below, out_row, 0)


def own_rows(h_ref, body, first=0, last=TAPS):
    def tap_row(a, carry):
        regs = load_taps(h_ref, a)

        def out_row(i, carry):
            body(regs, i + a - HALO, i)
            return carry

        return lax.fori_loop(jnp.maximum(0, HALO - a), jnp.minimum(ROWS, ROWS + HALO - a), out_row, carry)

    lax.fori_loop(first, last, tap_row, 0)


def side_outputs(parity):
    return range(COLS + HALO, WIDE) if parity else range(HALO)


def spectra_kernel(x_ref, tab_ref, h_ref, fr, fs, side_ref):
    place(forward(x_ref[...].reshape(ROWS * COLS, NT), tab_ref), 0, ROWS * COLS, fr, fs, 0)
    side_ref[...] = jnp.zeros_like(side_ref)

    def body(parity):
        inputs, outputs = side_columns(parity), side_outputs(parity)

        def out(regs, row, i):
            filter_row(regs, fr, fs, row * COLS, inputs, side_ref, i * HALO - outputs[0], outputs)

        own_rows(h_ref, out)

    each_parity(body)


def side_kernel(own_ref, near_ref, far_ref, tab_ref, h_ref, acc_ref, side_ref, nr, ns, fr, fs):
    keep = keep_of("inline")
    tiles = forward(jnp.concatenate([near_ref[...], far_ref[...]], axis=0), tab_ref)
    place(tiles, 0, HALO * COLS, nr, ns, 0)
    place([tile * keep for tile in tiles], HALO * COLS, HALO * HALO, fr, fs, 0)
    side_ref[...] = own_ref[...]
    far_below = parity_of("inline")

    def body(parity):
        inputs, outputs = side_columns(parity), side_outputs(parity)

        def near_out(regs, row, i):
            filter_row(regs, nr, ns, row * COLS, inputs, side_ref, i * HALO - outputs[0], outputs)

        def far_out(regs, row, i):
            base = row * HALO - inputs[0]
            filter_row(regs, fr, fs, base, inputs, side_ref, i * HALO - outputs[0], outputs)

        neighbour_rows(h_ref, 1 - far_below, near_out)
        neighbour_rows(h_ref, far_below, far_out)

    each_parity(body)


def halves(outputs):
    middle = len(outputs) // 2
    return outputs[:middle], outputs[middle:]


def inner_outputs(parity):
    return range(COLS + HALO) if parity else range(HALO, WIDE)


def ahead():
    place_in_run = lax.rem(lax.axis_index("xline"), 8)
    count = jnp.where((place_in_run == 1) | (place_in_run == 3), AHEAD[1], AHEAD[3])
    count = jnp.where(place_in_run == 0, AHEAD[0], count)
    return jnp.where(place_in_run == 5, AHEAD[2], count)


def filter_own(fr, fs, h_ref, acc_ref, first, last):
    def body(parity):
        def out(regs, row, i):
            for outputs in halves(inner_outputs(parity)):
                filter_row(regs, fr, fs, row * COLS, range(COLS), acc_ref, i * WIDE, outputs)

        own_rows(h_ref, out, first, last)

    each_parity(body)


def early_kernel(fr, fs, h_ref, acc_ref):
    acc_ref[...] = jnp.zeros_like(acc_ref)
    filter_own(fr, fs, h_ref, acc_ref, 0, ahead())


def late_kernel(acc_in, fr, fs, h_ref, acc_ref):
    acc_ref[...] = acc_in[...]
    filter_own(fr, fs, h_ref, acc_ref, ahead(), TAPS)


def near_kernel(acc_in, nr, ns, h_ref, inverse_ref, acc_ref):
    acc_ref[...] = acc_in[...]

    def body(parity):
        def out(regs, row, i):
            for outputs in halves(inner_outputs(parity)):
                filter_row(regs, nr, ns, row * COLS, range(COLS), acc_ref, i * WIDE, outputs)

        neighbour_rows(h_ref, 1 - parity_of("inline"), out)

    each_parity(body)


def mate_kernel(acc_ref, rest_ref, tab_ref, h_ref, mate_ref, fr, fs):
    keep = keep_of("inline")
    place([tile * keep for tile in forward(rest_ref[...], tab_ref)], 0, HALO * REST, fr, fs, 0)

    def body(parity):
        outputs, rest = side_outputs(1 - parity), other_columns(parity)
        inputs = side_columns(1 - parity)
        for i in range(ROWS):
            source = pl.ds((i * WIDE + outputs[0]) * 8, HALO * 8)
            mate_ref[pl.ds(i * HALO * 8, HALO * 8), :] = acc_ref[source, :]

        def out(regs, row, i):
            filter_row(regs, fr, fs, row * REST - rest[0], inputs, mate_ref, i * HALO - outputs[0], outputs)

        neighbour_rows(h_ref, parity_of("inline"), out)

    each_parity(body)


def inner_kernel(acc_ref, rr, rs, sr, ss, h_ref, out_ref):
    def body(parity):
        side, rest = side_columns(parity), other_columns(parity)
        for i in range(ROWS):
            out_ref[pl.ds(i * COLS * 8, COLS * 8), :] = acc_ref[pl.ds((i * WIDE + HALO) * 8, COLS * 8), :]

        def out(regs, row, i):
            for outputs in halves(range(HALO, HALO + COLS)):
                filter_row(regs, sr, ss, row * HALO - side[0], side, out_ref, i * COLS - HALO, outputs)
                filter_row(regs, rr, rs, row * REST - rest[0], rest, out_ref, i * COLS - HALO, outputs)

        neighbour_rows(h_ref, parity_of("inline"), out)

    each_parity(body)


def add_kernel(acc_ref, side_ref, out_ref):
    odd, keep = parity_of("xline"), keep_of("xline")
    out_ref[...] = acc_ref[...]
    for i in range(ROWS):
        target = pl.ds(pl.multiple_of((i * COLS + 12 * odd) * 8, 8), HALO * 8)
        out_ref[target, :] = out_ref[target, :] + side_ref[pl.ds(i * HALO * 8, HALO * 8), :] * keep


def inverse_kernel(acc_ref, mate_ref, tab_ref, out_ref, work):
    odd = parity_of("xline")
    work[...] = acc_ref[...]
    for i in range(ROWS):
        source = pl.ds(i * HALO * 8, HALO * 8)
        mate = pl.ds(pl.multiple_of((i * COLS + 12 - 12 * odd) * 8, 8), HALO * 8)
        work[mate, :] = work[mate, :] + mate_ref[source, :]
    lane = lax.broadcasted_iota(jnp.int32, (ROWS * COLS, 128), 1)
    parts = []
    for parity in (0, 1):
        tiles = [work[pl.ds(s, ROWS * COLS, stride=8), :] for s in SUBLANE[parity]]
        if parity == 0:
            tiles[0] = jnp.where(lane == 0, 0.5 * tiles[0], tiles[0])
        spectrum = jnp.concatenate(tiles, axis=1)
        parts.append(dot3(spectrum, tab_ref[2 * parity], tab_ref[2 * parity + 1]) * (2.0 / NT))
    out_ref[:, :, :HALF] = (parts[0] + parts[1]).reshape(ROWS, COLS, HALF)
    out_ref[:, :, HALF:] = (parts[0] - parts[1]).reshape(ROWS, COLS, HALF)


def call(kernel, outs, scratch, args, specs=None, weight=0):
    return pl.pallas_call(
        kernel,
        out_shape=[jax.ShapeDtypeStruct(shape, jnp.float32) for shape in outs],
        in_specs=specs or [pl.BlockSpec()] * len(args),
        scratch_shapes=[pltpu.VMEM(shape, jnp.float32) for shape in scratch],
        compiler_params=pltpu.CompilerParams(vmem_limit_bytes=40 * 2**20),
        cost_estimate=pl.CostEstimate(flops=weight * 10**9, bytes_accessed=0, transcendentals=0) if weight else None,
    )(*args)


def permutations(inline, xline):
    number = lambda i, j: i * xline + j
    side, far = [], []
    for i in range(inline):
        for j in range(xline):
            k = j - 1 if j % 2 == 0 else j + 1
            side.append((number(i, j), number(i, k) if 0 <= k < xline else number(i ^ 1, j)))
            k = i - 1 if i % 2 == 0 else i + 1
            far.append((number(i, j), number(k, j) if 0 <= k < inline else number(i, j ^ 1)))
    near = [(i, i ^ 1) for i in range(inline)]
    mate = [(j, j ^ 1) for j in range(xline)]
    return side, far, near, mate


def per_device(traces, filters):
    side, far, near, mate = permutations(lax.axis_size("inline"), lax.axis_size("xline"))
    tab, inverse_tab = (jnp.asarray(table) for table in tables())
    taps = jnp.transpose(filters.reshape(2, HALF // 128, 128, TAPS * TAPS), (3, 1, 0, 2)).reshape(-1, 128)

    corner, rest, rows = ((HALO * columns, NT) for columns in (HALO, REST, COLS))
    far_side, far_rest, near_rows = call(edges_kernel, [corner, rest, rows], [], (traces,), weight=2)
    far_side = lax.ppermute(far_side, AXES, far)
    near_rows = lax.ppermute(near_rows, "inline", near)
    far_rest = lax.ppermute(far_rest, AXES, far)

    wide = (ROWS * WIDE * 8, 128)
    frame = (ROWS * COLS * 8, 128)
    spot = (ROWS * HALO * 8, 128)
    side_frame = (HALO * HALO * 8, 128)
    rest_frame = (HALO * REST * 8, 128)
    rows_frame = (HALO * COLS * 8, 128)
    (h,) = call(taps_kernel, [(2 * TAPS * TAPS * 8, 128)], [], (taps,))
    fr, fs, to_side = call(spectra_kernel, [frame, frame, spot], [], (traces, tab, h))
    (acc,) = call(early_kernel, [wide], [], (fr, fs, h))
    vmem, anywhere = pl.BlockSpec(memory_space=pltpu.VMEM), pl.BlockSpec(memory_space=pl.ANY)
    to_side, nr, ns, sr, ss = call(
        side_kernel,
        [spot] + [rows_frame] * 2 + [side_frame] * 2,
        [],
        (to_side, near_rows, far_side, tab, h, acc),
        specs=[vmem] * 5 + [anywhere],
    )
    from_side = lax.ppermute(to_side, AXES, side)
    (acc,) = call(late_kernel, [wide], [], (acc, fr, fs, h), weight=20)
    (acc,) = call(near_kernel, [wide], [], (acc, nr, ns, h, inverse_tab))
    to_mate, rr, rs = call(mate_kernel, [spot, rest_frame, rest_frame], [], (acc, far_rest, tab, h))
    from_mate = lax.ppermute(to_mate, "xline", mate)
    (acc,) = call(inner_kernel, [frame], [], (acc, rr, rs, sr, ss, h), weight=1)
    (acc,) = call(add_kernel, [frame], [], (acc, from_side), weight=1)
    (out,) = call(inverse_kernel, [(ROWS, COLS, NT)], [frame], (acc, from_mate, inverse_tab))
    return out


def solution(mesh):
    return jax.shard_map(
        per_device,
        mesh=mesh,
        in_specs=(P("inline", "xline", None), P()),
        out_specs=P("inline", "xline", None),
        check_vma=False,
    )
```
